256 devices in a mesh: src: 8 (over x_hi, y), dst: 32 (over z, x_lo, core).
Axes of the slice: x: 4 (x_hi: 2, x_lo: 2; x = x_hi * 2 + x_lo), y: 4, z: 8, core: 2. Of those that a mesh axis runs over, the one named last changes fastest.
Arguments:
- src_rows: float32 [131072, 200], P(('src', 'dst')), may hold values from -10 to 10
- src_state: float32 [131072], P(('src', 'dst')), may hold values from 0.02 to 2
- dst_rows: float32 [131072, 200], P(('src', 'dst')), may hold values from -10 to 10
- dst_state: float32 [131072], P(('src', 'dst')), may hold values from 0.02 to 2
- relations: float32 [1024, 200], replicated, may hold values from 0.1 to 1.9
- relation_state: float32 [1024], replicated, may hold values from 1 to 100
- block_tiles: int32 [2, 4096, 2], P(None, ('src', 'dst')), may hold values from 0 to 3
- src_offsets: int32 [2, 4096, 128], P(None, ('src', 'dst')), may hold values from 0 to 127
- dst_offsets: int32 [2, 4096, 128], P(None, ('src', 'dst')), may hold values from 0 to 127
- relation_ids: int32 [2, 4096, 128], P(None, ('src', 'dst')), may hold values from 0 to 1023
- negative_ids: int32 [2, 4096, 50], P(None, ('src', 'dst')), may hold values from 0 to 511
Outputs:
- src_out: float32 [131072, 200], P(('src', 'dst'))
- dst_out: float32 [131072, 200], P(('src', 'dst'))
- rel_out: float32 [1024, 200], replicated
The draws below stay inside these ranges and needn't reach their ends.
Inputs may be any that keep to these rules, and one draw needn't show every extreme that they name: `block_tiles`: entry 0 names the block's tile of 128 source rows, entry 1 its tile of 128 slab rows, both within the partition; all edges of a block lie in these two tiles. `negative_ids`: rows within the slab held in that round.
All inputs are finite; a program needn't handle non-finite values.
Results may differ from the reference program's by a relative error of at most 0.0001.
Values sent between devices are 32-bit elements; how exact they have to be, the bound alone decides.
A program may use at most 64 MiB of HBM per device.

```python
import math
import jax
import jax.numpy as jnp
import numpy as np
from jax import lax

D = 200
REL = 1024
TILE = 128
NEG = 50
ROUNDS = 2
ROWS_DEV = 512
BLK = 16
ENTITIES = 131072
EDGE_BLOCKS = 4096
N_SRC = 8
N_DST = 32


def scale_entries(key_scale, values, row_ratio):
    key_rows, key_cols = jax.random.split(key_scale)
    row_scale = 0.5 * jnp.exp(jax.random.uniform(key_rows, (values.shape[0], 1), jnp.float32) * math.log(row_ratio))
    col_scale = 0.05 * jnp.exp(jax.random.uniform(key_cols, (1, values.shape[1]), jnp.float32) * math.log(10.0))
    return values * row_scale * col_scale


def draw_src_rows(key, part):
    key = jax.random.fold_in(key, 11)
    key_vals = jax.random.fold_in(key, 0)
    key_scale = jax.random.fold_in(key, 2)
    values = jnp.clip(jax.random.normal(key_vals, (ENTITIES, D), jnp.float32), -4.0, 4.0)
    return scale_entries(key_scale, values, 10.0)


def draw_dst_rows(key, part):
    key = jax.random.fold_in(key, 12)
    key_vals = jax.random.fold_in(key, 0)
    key_scale = jax.random.fold_in(key, 2)
    values = jnp.clip(jax.random.normal(key_vals, (ENTITIES, D), jnp.float32), -4.0, 4.0)
    return scale_entries(key_scale, values, 10.0)


def with_ends(drawn, rng, low, top_value):
    longest = drawn.shape.index(max(drawn.shape))
    spots = []
    for shift in (0, 1):
        where = [jax.random.randint(jax.random.fold_in(rng, axis), (), 0, length) for axis, length in enumerate(drawn.shape)]
        where[longest] = (where[longest] + shift) % drawn.shape[longest]
        spots.append(tuple(where))
    return drawn.at[spots[0]].set(low).at[spots[1]].set(top_value)


def shard_levels(own_key, shape, cuts, low, high):
    gain, own = 1.0, jax.random.fold_in(own_key, 6)
    for axis_at, blocks in cuts:
        steps = jnp.exp(jax.random.uniform(jax.random.fold_in(own, axis_at), (blocks,), jnp.float32, low / len(cuts), high / len(cuts)))
        gain = gain * jnp.repeat(steps, shape[axis_at] // blocks).reshape([-1 if axis == axis_at else 1 for axis in range(len(shape))])
    return gain


def rank_table(amount, lean):
    loads = [(1 << 20) // math.isqrt(grade ** lean) + 1 for grade in range(1, amount + 1)]
    scale = 1 + sum(loads) // (1 << 30)
    return np.cumsum(np.array([max(1, weight // scale) for weight in loads]))


def skewed_ids(stream_key, shape, count, slope):
    grid = rank_table(count, slope)
    pick = jax.random.randint(jax.random.fold_in(stream_key, 1), shape, 0, int(grid[count - 1]))
    grade = jnp.searchsorted(jnp.asarray(grid, jnp.int32), pick, side="right")
    return jax.random.permutation(jax.random.fold_in(stream_key, 2), count)[grade].astype(jnp.int32)


def setup_inputs(seed: int = 0) -> dict:
    seeds = jax.random.split(jax.random.key(seed), 12)
    return {
        "src_rows": draw_src_rows(jax.random.fold_in(seeds[11], 71), 0),
        "src_state": jnp.clip(jnp.exp(math.log(2.0) - 4.6051702 * jax.random.uniform(seeds[1], (ENTITIES,), jnp.float32) ** shard_levels(seeds[1], (ENTITIES,), ((0, 256),), -0.2, 0.2)), 0.02, 2.0),
        "dst_rows": draw_dst_rows(jax.random.fold_in(seeds[11], 71), 0),
        "dst_state": jnp.clip(jnp.exp(math.log(2.0) - 4.6051702 * jax.random.uniform(seeds[3], (ENTITIES,), jnp.float32) ** shard_levels(seeds[3], (ENTITIES,), ((0, 256),), -0.2, 0.2)), 0.02, 2.0),
        "relations": jnp.clip(1.0 + 0.18 * jax.random.normal(seeds[4], (REL, D), jnp.float32), 0.1, 1.9),
        "relation_state": jnp.clip(jnp.exp(jax.random.uniform(seeds[5], (REL,), jnp.float32, math.log(1.0), math.log(100.0))), 1.0, 100.0),
        "block_tiles": with_ends(jax.random.randint(seeds[6], (ROUNDS, EDGE_BLOCKS, 2), 0, ROWS_DEV // TILE), jax.random.fold_in(seeds[6], 1), 0, (ROWS_DEV // TILE) - 1).astype(jnp.int32),
        "src_offsets": with_ends(jax.random.randint(seeds[7], (ROUNDS, EDGE_BLOCKS, TILE), 0, TILE), jax.random.fold_in(seeds[7], 1), 0, TILE - 1).astype(jnp.int32),
        "dst_offsets": with_ends(jax.random.randint(seeds[8], (ROUNDS, EDGE_BLOCKS, TILE), 0, TILE), jax.random.fold_in(seeds[8], 1), 0, TILE - 1).astype(jnp.int32),
        "relation_ids": with_ends(skewed_ids(seeds[9], (ROUNDS, EDGE_BLOCKS, TILE), REL, 2), jax.random.fold_in(seeds[9], 3), 0, REL - 1).astype(jnp.int32),
        "negative_ids": with_ends(jax.random.randint(seeds[10], (ROUNDS, EDGE_BLOCKS, NEG), 0, ROWS_DEV), jax.random.fold_in(seeds[10], 1), 0, ROWS_DEV - 1).astype(jnp.int32),
    }


learn_rate = 0.1
highest = lax.Precision.HIGHEST

def adagrad(entries, squares, gradient):
    new_squares = squares + lax.optimization_barrier(jnp.mean(gradient * gradient, axis=-1))
    return (entries - learn_rate * gradient / jnp.sqrt(new_squares)[:, None], new_squares)

def partition_terms(sources, slab, rel_table, tile_ids, src_off, dst_off, rel_ids, neg_ids):
    src_index = tile_ids[:, 0:1] * TILE + src_off
    dst_index = tile_ids[:, 1:2] * TILE + dst_off
    head_rows = sources[src_index]
    tail_rows = slab[dst_index]
    diagonal = rel_table[rel_ids]
    neg_rows = slab[neg_ids]
    lifted = head_rows * diagonal
    positive = lax.optimization_barrier(jnp.sum(lifted * tail_rows, axis=-1))
    negative = jnp.einsum('bed,bnd->ben', lifted, neg_rows, precision=highest)
    pos_weight = -jax.nn.sigmoid(-positive)
    neg_weight = jax.nn.sigmoid(negative) / NEG
    pulled = pos_weight[..., None] * tail_rows + jnp.einsum('ben,bnd->bed', neg_weight, neg_rows, precision=highest)
    head_grad = pulled * diagonal
    diag_grad = pulled * head_rows
    tail_grad = pos_weight[..., None] * lifted
    neg_grad = jnp.einsum('ben,bed->bnd', neg_weight, lifted, precision=highest)
    src_grad = jnp.zeros_like(sources).at[src_index.reshape(-1)].add(head_grad.reshape(-1, D))
    slab_grad = jnp.zeros_like(slab).at[dst_index.reshape(-1)].add(tail_grad.reshape(-1, D))
    slab_grad = slab_grad.at[neg_ids.reshape(-1)].add(neg_grad.reshape(-1, D))
    rel_grad = jnp.zeros_like(rel_table).at[rel_ids.reshape(-1)].add(diag_grad.reshape(-1, D))
    return (src_grad, slab_grad, rel_grad)

def reference(src_rows, src_state, dst_rows, dst_state, relations, relation_state, block_tiles, src_offsets, dst_offsets, relation_ids, negative_ids):
    part_count = N_SRC * N_DST
    sources = src_rows.reshape(part_count, ROWS_DEV, D)
    source_sq = src_state.reshape(part_count, ROWS_DEV)
    held = dst_rows.reshape(part_count, ROWS_DEV, D)
    held_sq = dst_state.reshape(part_count, ROWS_DEV)
    rel_table = relations
    rel_sq = relation_state
    for round_index in range(ROUNDS):
        tiles_now = block_tiles[round_index].reshape(part_count, BLK, 2)
        src_now = src_offsets[round_index].reshape(part_count, BLK, TILE)
        dst_now = dst_offsets[round_index].reshape(part_count, BLK, TILE)
        rel_now = relation_ids[round_index].reshape(part_count, BLK, TILE)
        neg_now = negative_ids[round_index].reshape(part_count, BLK, NEG)
        current_rel = rel_table

        def one_part(rel_total, pieces):
            src_part, src_part_sq, slab, slab_sq, tile_ids, src_off, dst_off, rel_ids, neg_ids = pieces
            src_grad, slab_grad, rel_grad = partition_terms(src_part, slab, current_rel, tile_ids, src_off, dst_off, rel_ids, neg_ids)
            new_src, new_src_sq = adagrad(src_part, src_part_sq, src_grad)
            new_slab, new_slab_sq = adagrad(slab, slab_sq, slab_grad)
            return (rel_total + rel_grad, (new_src, new_src_sq, new_slab, new_slab_sq))
        rel_total, outputs = lax.scan(one_part, jnp.zeros_like(rel_table), (sources, source_sq, held, held_sq, tiles_now, src_now, dst_now, rel_now, neg_now))
        sources, source_sq, held, held_sq = outputs
        rel_table, rel_sq = adagrad(rel_table, rel_sq, rel_total)
        held = jnp.roll(held.reshape(N_SRC, N_DST, ROWS_DEV, D), 1, axis=1).reshape(part_count, ROWS_DEV, D)
        held_sq = jnp.roll(held_sq.reshape(N_SRC, N_DST, ROWS_DEV), 1, axis=1).reshape(part_count, ROWS_DEV)
    return (sources.reshape(part_count * ROWS_DEV, D), held.reshape(part_count * ROWS_DEV, D), rel_table)
```

```python
import functools

import jax
import jax.numpy as jnp
from jax import lax
from jax.experimental import pallas as pl
from jax.experimental.pallas import tpu as pltpu
from jax.sharding import PartitionSpec as P

MESH = pl.DeviceIdType.MESH
f32, bf16, i32 = jnp.float32, jnp.bfloat16, jnp.int32
learn_rate = 0.1
D, REL, TILE, NEG, ROWS, BLK, ROUNDS = 200, 1024, 128, 50, 512, 16, 2
HALF = REL // 2
EDGES = BLK * TILE
NEGS = BLK * 64
VMEM_LIMIT = 56 << 20


def two_parts(value):
    high = value.astype(bf16)
    return high, (value - high.astype(f32)).astype(bf16)


def stacked(value):
    return jnp.concatenate(two_parts(value), axis=0)


def folded(value):
    half = value.shape[0] // 2
    return value[:half] + value[half:]


def dot(a, b, dims=((1,), (0,))):
    return lax.dot_general(a, b, (dims, ((), ())), preferred_element_type=f32)


NT = ((1,), (1,))
TN = ((0,), (0,))


def lane_pick(tile, offsets):
    index = jnp.broadcast_to(offsets, tile.shape)
    return jnp.take_along_axis(tile, index, axis=1, mode="promise_in_bounds")


def one_hot(ids, rows):
    places = lax.broadcasted_iota(i32, (rows, ids.shape[1]), 0)
    return jnp.where(places == ids, 1.0, 0.0).astype(bf16)


def adagrad(table, sums, grad):
    sums = sums + jnp.sum(grad * grad, axis=0, keepdims=True) * (1.0 / D)
    return table - grad * (learn_rate / jnp.sqrt(sums)), sums


def round_kernel(
    rnd,
    tiles_ref,
    src_ref,
    src_sq_ref,
    slab_ref,
    slab_sq_ref,
    rel_ref,
    src_off_ref,
    dst_off_ref,
    rel_ids_ref,
    neg_ids_ref,
    new_src_ref,
    new_src_sq_ref,
    new_slab_ref,
    new_slab_sq_ref,
    rel_grad_ref,
    rel_parts,
    rel_hot,
    src_hot,
    slab_hot,
    negs,
    src_terms,
    slab_terms,
    rel_terms,
):
    rel_parts[...] = stacked(rel_ref[...])
    slab_parts = stacked(slab_ref[...])
    for p in range(4):
        lanes = pl.ds(p * 256, 256)
        ids = jnp.concatenate(
            [neg_ids_ref[rnd, 2 * p : 2 * p + 1, :], neg_ids_ref[rnd, 2 * p + 1 : 2 * p + 2, :]], axis=1
        )
        hot = one_hot(ids, ROWS)
        slab_hot[:, pl.ds(EDGES + p * 256, 256)] = hot
        negs[:, lanes] = folded(dot(slab_parts, hot))

    def pair(p, carry):
        heads, tails, hots = [], [], []
        for j in range(2):
            b = 2 * p + j
            src_tile = tiles_ref[(rnd * BLK + b) * 2]
            dst_tile = tiles_ref[(rnd * BLK + b) * 2 + 1]
            src_off = src_off_ref[rnd, pl.ds(b, 1), :]
            dst_off = dst_off_ref[rnd, pl.ds(b, 1), :]
            heads.append(lane_pick(src_ref[:, pl.ds(pl.multiple_of(src_tile * TILE, TILE), TILE)], src_off))
            tails.append(lane_pick(slab_ref[:, pl.ds(pl.multiple_of(dst_tile * TILE, TILE), TILE)], dst_off))
            own = pl.ds(pl.multiple_of(b * TILE, TILE), TILE)
            src_hot[:, own] = one_hot(src_off + src_tile * TILE, ROWS)
            slab_hot[:, own] = one_hot(dst_off + dst_tile * TILE, ROWS)
            hots.append(one_hot(rel_ids_ref[rnd, pl.ds(b, 1), :], REL))
        head = jnp.concatenate(heads, axis=1)
        tail = jnp.concatenate(tails, axis=1)
        hot = jnp.concatenate(hots, axis=1)
        both = pl.ds(pl.multiple_of(p * 256, 256), 256)
        rel_hot[:, both] = hot
        diagonal = folded(dot(rel_parts[...], hot))
        lifted = head * diagonal
        lifted_high, lifted_low = two_parts(lifted)
        own_negs = negs[:, pl.ds(pl.multiple_of(p * 128, 128), 128)]
        neg_high, neg_low = two_parts(own_negs)
        positive = jnp.sum(lifted * tail, axis=0, keepdims=True)
        score = (
            dot(neg_high, lifted_high, TN) + dot(neg_low, lifted_high, TN) + dot(neg_high, lifted_low, TN)
        )
        pos_weight = -jax.nn.sigmoid(-positive)
        first = jax.nn.sigmoid(score[:64, :128]) * (1.0 / NEG)
        second = jax.nn.sigmoid(score[64:, 128:]) * (1.0 / NEG)
        nothing = jnp.zeros((64, 128), f32)
        weight = jnp.concatenate(
            [jnp.concatenate([first, nothing], axis=1), jnp.concatenate([nothing, second], axis=1)], axis=0
        )
        weight_high, weight_low = two_parts(weight)
        pulled = (
            pos_weight * tail
            + folded(dot(jnp.concatenate([neg_high, neg_low], axis=0), weight_high))
            + dot(neg_high, weight_low)
        )
        neg_grad = folded(dot(jnp.concatenate([lifted_high, lifted_low], axis=0), weight_high, NT)) + dot(
            lifted_high, weight_low, NT
        )
        src_terms[:, both] = stacked(pulled * diagonal)
        rel_terms[:, both] = stacked(pulled * head)
        slab_terms[:, both] = stacked(pos_weight * lifted)
        slab_terms[:, pl.ds(pl.multiple_of(EDGES + p * 128, 128), 128)] = stacked(neg_grad)
        return carry

    lax.fori_loop(0, BLK // 2, pair, 0)

    def rel_chunk(q, carry):
        rows = pl.ds(pl.multiple_of(q * 256, 256), 256)
        rel_grad_ref[:, rows] = folded(dot(rel_terms[...], rel_hot[rows, :], NT))
        return carry

    lax.fori_loop(0, REL // 256, rel_chunk, 0)

    def row_chunk(q, carry):
        rows = pl.ds(pl.multiple_of(q * 256, 256), 256)
        grad = folded(dot(src_terms[...], src_hot[rows, :], NT))
        new_src_ref[:, rows], new_src_sq_ref[:, rows] = adagrad(src_ref[:, rows], src_sq_ref[:, rows], grad)
        grad = folded(dot(slab_terms[...], slab_hot[rows, :], NT))
        new_slab_ref[:, rows], new_slab_sq_ref[:, rows] = adagrad(slab_ref[:, rows], slab_sq_ref[:, rows], grad)
        return carry

    lax.fori_loop(0, ROWS // 256, row_chunk, 0)


def run_round(rnd, tiles, src, src_sq, slab, slab_sq, rel, src_off, dst_off, rel_ids, neg_ids):
    vmem = pl.BlockSpec(memory_space=pltpu.VMEM)
    return pl.pallas_call(
        functools.partial(round_kernel, rnd),
        out_shape=[
            jax.ShapeDtypeStruct((D, ROWS), f32),
            jax.ShapeDtypeStruct((1, ROWS), f32),
            jax.ShapeDtypeStruct((D, ROWS), f32),
            jax.ShapeDtypeStruct((1, ROWS), f32),
            jax.ShapeDtypeStruct((D, REL), f32),
        ],
        in_specs=[pl.BlockSpec(memory_space=pltpu.SMEM)] + [vmem] * 9,
        out_specs=[vmem] * 5,
        scratch_shapes=[
            pltpu.VMEM((2 * D, REL), bf16),
            pltpu.VMEM((REL, EDGES), bf16),
            pltpu.VMEM((ROWS, EDGES), bf16),
            pltpu.VMEM((ROWS, EDGES + NEGS), bf16),
            pltpu.VMEM((D, NEGS), f32),
            pltpu.VMEM((2 * D, EDGES), bf16),
            pltpu.VMEM((2 * D, EDGES + NEGS), bf16),
            pltpu.VMEM((2 * D, EDGES), bf16),
        ],
        compiler_params=pltpu.CompilerParams(vmem_limit_bytes=VMEM_LIMIT),
        name=f"round{rnd}",
    )(tiles, src, src_sq, slab, slab_sq, rel, src_off, dst_off, rel_ids, neg_ids)


def exchange_kernel(
    grad_ref,
    rel_ref,
    rel_sq_ref,
    slab_ref,
    slab_sq_ref,
    new_rel_ref,
    new_rel_sq_ref,
    moved_ref,
    moved_sq_ref,
    land0,
    acc,
    land1,
    mid,
    land2,
    tot,
    part,
    gath,
    peer_half,
    grad,
    ss,
    rs,
):
    s, c = lax.axis_index("src"), lax.axis_index("dst")
    core, low, z = c % 2, (c // 2) % 2, c // 4
    g = s * 2 + low

    def in_plane(k):
        return (k // 2, (z * 2 + k % 2) * 2 + core)

    def along_z(k):
        return (s, (k * 2 + low) * 2 + core)

    peer = (s, c + 1 - 2 * core)
    right, left = (s, (c + 1) % 32), (s, (c + 31) % 32)

    def send(src, dst, n, device):
        copy = pltpu.make_async_remote_copy(
            src, dst, ss.at[n], rs.at[n], device_id=device, device_id_type=MESH
        )
        copy.start()
        return copy

    def wait_for(ref, sem):
        pltpu.make_async_copy(ref, ref, sem).wait()

    barrier = pltpu.get_barrier_semaphore()
    pl.semaphore_signal(barrier, inc=1, device_id=peer, device_id_type=MESH)
    pl.semaphore_signal(barrier, inc=1, device_id=left, device_id_type=MESH)
    for i in range(1, 16):
        pl.semaphore_signal(barrier, inc=1, device_id=in_plane((g + i) % 16), device_id_type=MESH)
    for i in range(1, 8):
        pl.semaphore_signal(barrier, inc=1, device_id=along_z((z + i) % 8), device_id_type=MESH)
    pl.semaphore_wait(barrier, 24)

    give = pl.ds(pl.multiple_of((1 - core) * HALF, 128), HALF)
    send(grad_ref.at[:, give], land0, 0, peer).wait()
    for k in range(100):
        rows, lane = slice(k // 4 * 8, k // 4 * 8 + 8), k % 4 * 128
        acc[k] = grad_ref[rows, pl.ds(pl.multiple_of(core * HALF + lane, 128), 128)] + land0[rows, lane : lane + 128]
    acc[100:112] = jnp.zeros((12, 8, 128), f32)
    for i in range(1, 16):
        k = (g + i) % 16
        send(acc.at[pl.ds(k * 7, 7)], land1.at[i - 1], 1, in_plane(k))
    hop = send(slab_ref, moved_ref, 6, right)
    hop_sq = send(slab_sq_ref, moved_sq_ref, 7, right)
    wait_for(land1, rs.at[1])
    mid[0:7] = acc[pl.ds(g * 7, 7)] + jnp.sum(land1[...], axis=0)
    mid[7:8] = jnp.zeros((1, 8, 128), f32)
    for i in range(1, 8):
        k = (z + i) % 8
        send(mid.at[k], land2.at[i - 1], 2, along_z(k))
    wait_for(land2, rs.at[2])
    tot[...] = mid[z] + jnp.sum(land2[...], axis=0)
    part[z] = tot[...]
    for i in range(1, 8):
        send(tot, part.at[z], 3, along_z((z + i) % 8))
    wait_for(land2, rs.at[3])
    for i in range(1, 16):
        send(part.at[pl.ds(0, 7)], gath.at[pl.ds(g * 7, 7)], 4, in_plane((g + i) % 16))
    gath[pl.ds(g * 7, 7)] = part[0:7]
    wait_for(land1, rs.at[4])
    swap = send(gath.at[pl.ds(0, 100)], peer_half, 5, peer)
    for k in range(100):
        rows, lane = slice(k // 4 * 8, k // 4 * 8 + 8), k % 4 * 128
        grad[rows, pl.ds(pl.multiple_of(core * HALF + lane, 128), 128)] = gath[k]
    swap.wait_recv()
    for k in range(100):
        rows, lane = slice(k // 4 * 8, k // 4 * 8 + 8), k % 4 * 128
        grad[rows, pl.ds(pl.multiple_of((1 - core) * HALF + lane, 128), 128)] = peer_half[k]
    new_rel_ref[...], new_rel_sq_ref[...] = adagrad(rel_ref[...], rel_sq_ref[...], grad[...])
    swap.wait_send()
    wait_for(land1, ss.at[1])
    wait_for(land2, ss.at[2])
    wait_for(land2, ss.at[3])
    wait_for(land1, ss.at[4])
    hop.wait()
    hop_sq.wait()


def exchange(rnd, grad, rel, rel_sq, slab, slab_sq):
    vmem = pl.BlockSpec(memory_space=pltpu.VMEM)

    def held(*shape):
        return pltpu.VMEM(shape, f32)

    return pl.pallas_call(
        exchange_kernel,
        out_shape=[
            jax.ShapeDtypeStruct((D, REL), f32),
            jax.ShapeDtypeStruct((1, REL), f32),
            jax.ShapeDtypeStruct((D, ROWS), f32),
            jax.ShapeDtypeStruct((1, ROWS), f32),
        ],
        in_specs=[vmem] * 5,
        out_specs=[vmem] * 4,
        scratch_shapes=[
            held(D, HALF),
            held(112, 8, 128),
            held(15, 7, 8, 128),
            held(8, 8, 128),
            held(7, 8, 128),
            held(8, 128),
            held(8, 8, 128),
            held(112, 8, 128),
            held(100, 8, 128),
            held(D, REL),
            pltpu.SemaphoreType.DMA((8,)),
            pltpu.SemaphoreType.DMA((8,)),
        ],
        compiler_params=pltpu.CompilerParams(
            collective_id=rnd, has_side_effects=True, vmem_limit_bytes=VMEM_LIMIT
        ),
        name=f"exchange{rnd}",
    )(grad, rel, rel_sq, slab, slab_sq)


def shards(
    src_rows,
    src_state,
    dst_rows,
    dst_state,
    relations,
    relation_state,
    block_tiles,
    src_offsets,
    dst_offsets,
    relation_ids,
    negative_ids,
):
    src, slab, rel = src_rows.T, dst_rows.T, relations.T
    src_sq, slab_sq, rel_sq = src_state[None, :], dst_state[None, :], relation_state[None, :]
    tiles = block_tiles.reshape(-1)
    neg_ids = jnp.pad(negative_ids, ((0, 0), (0, 0), (0, 64 - NEG)), constant_values=-1).reshape(
        ROUNDS, BLK // 2, 128
    )
    for rnd in range(ROUNDS):
        src, src_sq, slab, slab_sq, grad = run_round(
            rnd, tiles, src, src_sq, slab, slab_sq, rel, src_offsets, dst_offsets, relation_ids, neg_ids
        )
        rel, rel_sq, slab, slab_sq = exchange(rnd, grad, rel, rel_sq, slab, slab_sq)
    return src.T, slab.T, rel.T


def solution(mesh):
    own = ("src", "dst")
    ids = P(None, own, None)
    return jax.shard_map(
        shards,
        mesh=mesh,
        in_specs=(P(own, None), P(own), P(own, None), P(own), P(), P(), ids, ids, ids, ids, ids),
        out_specs=(P(own, None), P(own, None), P()),
        check_vma=False,
    )
```

```python
import jax
import jax.numpy as jnp
from jax import lax
from jax.experimental import pallas as pl
from jax.experimental.pallas import tpu as pltpu
from jax.sharding import PartitionSpec as P

MESH = pl.DeviceIdType.MESH
f32, bf16, i32 = jnp.float32, jnp.bfloat16, jnp.int32
learn_rate = 0.1
D, REL, TILE, NEG, ROWS, BLK, ROUNDS = 200, 1024, 128, 50, 512, 16, 2
EDGES = BLK * TILE
NEGS = BLK * 64
FEATS = D // 8
SHARE = 7
SHARES = 16 * SHARE
HALF_TILES = 4 * FEATS
VMEM_LIMIT = 60 << 20
NT = ((1,), (1,))
TN = ((0,), (0,))


def two_parts(value):
    high = value.astype(bf16)
    return high, (value - high.astype(f32)).astype(bf16)


def stacked(value):
    return jnp.concatenate(two_parts(value), axis=0)


def folded(value):
    half = value.shape[0] // 2
    return value[:half] + value[half:]


def dot(a, b, dims=((1,), (0,))):
    return lax.dot_general(a, b, (dims, ((), ())), preferred_element_type=f32)


def one_hot(ids, rows):
    places = lax.broadcasted_iota(i32, (rows, ids.shape[1]), 0)
    return jnp.where(places == ids, 1.0, 0.0).astype(bf16)


def adagrad(table, sums, grad):
    sums = sums + jnp.sum(grad * grad, axis=0, keepdims=True) * (1.0 / D)
    return table - grad * (learn_rate / jnp.sqrt(sums)), sums


def lanes_at(start, size):
    return pl.ds(start if isinstance(start, int) else pl.multiple_of(start, size), size)


def as_column(row):
    size = row.shape[1]
    square = lax.broadcasted_iota(i32, (size, size), 0) == lax.broadcasted_iota(i32, (size, size), 1)
    return jnp.sum(jnp.where(square, row.astype(f32), 0.0), axis=1, keepdims=True).astype(i32)


def place_ids(m):
    for rnd in range(ROUNDS):
        tiles = m.tiles[rnd]
        m.src_ids[rnd] = m.src_off[rnd] + as_column(tiles[0:1]) * TILE
        m.dst_ids[rnd] = m.dst_off[rnd] + as_column(tiles[1:2]) * TILE


def gather_negatives(rnd, m):
    ids = m.neg_ids[rnd]
    ids = jnp.concatenate([ids, jnp.full((BLK, 64 - NEG), -1, i32)], axis=1)
    for p in range(4):
        row = jnp.concatenate([ids[4 * p + j : 4 * p + j + 1, :] for j in range(4)], axis=1)
        hot = one_hot(row, ROWS)
        m.slab_hot[:, pl.ds(EDGES + p * 256, 256)] = hot
        negs = folded(dot(m.slab_parts[...], hot))
        here = pl.ds(p * 256, 256)
        m.neg_parts[:, here] = stacked(negs)
        for part, value in enumerate(two_parts(negs.T)):
            m.negs_turned[part, here, :] = value


def pair_ids(ref, rnd, p):
    return jnp.concatenate([ref[rnd, pl.ds(2 * p + j, 1), :] for j in range(2)], axis=1)


def gather_pair(rnd, m, p):
    both = lanes_at(p * 256, 256)
    src_hot = one_hot(pair_ids(m.src_ids, rnd, p), ROWS)
    dst_hot = one_hot(pair_ids(m.dst_ids, rnd, p), ROWS)
    m.src_hot[:, both] = src_hot
    m.slab_hot[:, both] = dst_hot
    m.heads[:, both] = folded(dot(m.src_parts[...], src_hot))
    m.tails[:, both] = folded(dot(m.slab_parts[...], dst_hot))
    m.rel_hot[:, both] = one_hot(pair_ids(m.rel_ids, rnd, p), REL)


def group_terms(m, first, count):
    pairs = range(count)
    both = [lanes_at((first + i) * 256, 256) for i in pairs]
    own = [lanes_at((first + i) * 128, 128) for i in pairs]
    lifted, parts, neg, score, weight = [], [], [], [], []
    for i in pairs:
        diagonal = folded(dot(m.rel_parts[...], m.rel_hot[:, both[i]]))
        m.diagonals[:, both[i]] = diagonal
        lifted.append(m.heads[:, both[i]] * diagonal)
        parts.append(two_parts(lifted[i]))
    for i in pairs:
        high, low = parts[i]
        turned = m.negs_turned[:, own[i], :]
        score.append(dot(turned.reshape(256, D), high))
        score[i] = folded(score[i]) + dot(turned[0], low)
    for i in pairs:
        pieces = [jax.nn.sigmoid(score[i][64 * j : 64 * j + 64, 128 * j : 128 * j + 128]) * (1.0 / NEG) for j in range(2)]
        nothing = jnp.zeros((64, 128), f32)
        weight.append(
            two_parts(
                jnp.concatenate(
                    [jnp.concatenate([pieces[0], nothing], axis=1), jnp.concatenate([nothing, pieces[1]], axis=1)], axis=0
                )
            )
        )
    for i in pairs:
        head, tail = m.heads[:, both[i]], m.tails[:, both[i]]
        negs = m.neg_parts[:, own[i]]
        positive = jnp.sum(lifted[i] * tail, axis=0, keepdims=True)
        pos_weight = -jax.nn.sigmoid(-positive)
        pulled = pos_weight * tail + folded(dot(negs, weight[i][0])) + dot(negs[:D], weight[i][1])
        m.src_terms[:, both[i]] = stacked(pulled * m.diagonals[:, both[i]])
        m.rel_terms[:, both[i]] = stacked(pulled * head)
        m.slab_terms[:, both[i]] = stacked(pos_weight * lifted[i])
    for i in pairs:
        neg_grad = folded(dot(jnp.concatenate(parts[i], axis=0), weight[i][0], NT)) + dot(parts[i][0], weight[i][1], NT)
        m.slab_terms[:, lanes_at(EDGES + (first + i) * 128, 128)] = stacked(neg_grad)


GROUP = 8


def all_terms(m):
    for i in range(BLK // 2 // GROUP):
        group_terms(m, i * GROUP, GROUP)


def gather_all(rnd, m):
    for p in range(BLK // 2):
        gather_pair(rnd, m, p)


def rel_gradient(m, out, half):
    for q in range(2):
        rows = lanes_at(half * (REL // 2) + q * 256, 256)
        grad = folded(dot(m.rel_terms[...], m.rel_hot[rows, :], NT))
        for j in range(2):
            piece = grad[:, j * 128 : j * 128 + 128]
            out[half, pl.ds((2 * q + j) * FEATS, FEATS)] = piece.reshape(FEATS, 8, 128)


def row_update(terms, hot, table, sums, new_table, new_sums, q):
    rows = pl.ds(q * 256, 256)
    grad = folded(dot(terms[...], hot[rows, :], NT))
    new_table[:, rows], new_sums[:, rows] = adagrad(table[:, rows], sums[:, rows], grad)


def rel_update(m, half, table, sums, grad, new_table, new_sums):
    for j in range(4):
        rows = lanes_at(half * (REL // 2) + j * 128, 128)
        piece = grad[half, pl.ds(j * FEATS, FEATS)].reshape(D, 128)
        new, new_sq = adagrad(table[:, rows], sums[:, rows], piece)
        new_table[:, rows] = new
        if new_sums is not None:
            new_sums[:, rows] = new_sq
            m.rel_parts[:, rows] = stacked(new)


PLANE = sorted(
    ((dx, dy) for dx in range(4) for dy in range(4) if dx or dy),
    key=lambda step: -min(step[0], 4 - step[0]) - min(step[1], 4 - step[1]),
)


class Refs:
    def __init__(self, names, refs):
        for name, ref in zip(names, refs, strict=True):
            setattr(self, name, ref)


INPUTS = (
    ("tiles", "src0", "src_sq0", "slab0", "slab_sq0", "rel0", "rel_sq0")
    + ("src_off", "dst_off", "rel_ids", "neg_ids")
)
OUTPUTS = ("src2", "slab_out", "rel2")
SCRATCH = {
    "src_ids": ((ROUNDS, BLK, TILE), i32),
    "dst_ids": ((ROUNDS, BLK, TILE), i32),
    "src_parts": ((2 * D, ROWS), bf16),
    "slab_parts": ((2 * D, ROWS), bf16),
    "rel_parts": ((2 * D, REL), bf16),
    "rel_hot": ((REL, EDGES), bf16),
    "src_hot": ((ROWS, EDGES), bf16),
    "slab_hot": ((ROWS, EDGES + NEGS), bf16),
    "neg_parts": ((2 * D, NEGS), bf16),
    "negs_turned": ((2, NEGS, D), bf16),
    "diagonals": ((D, EDGES), f32),
    "heads": ((D, EDGES), f32),
    "tails": ((D, EDGES), f32),
    "src_terms": ((2 * D, EDGES), bf16),
    "slab_terms": ((2 * D, EDGES + NEGS), bf16),
    "rel_terms": ((2 * D, EDGES), bf16),
    "src1": ((D, ROWS), f32),
    "src_sq1": ((1, ROWS), f32),
    "src_sq2": ((1, ROWS), f32),
    "rel1": ((D, REL), f32),
    "rel_sq1": ((1, REL), f32),
    "slab_new": ((2, D, ROWS), f32),
    "slab_sq_new": ((2, 1, ROWS), f32),
    "slab1": ((D, ROWS), f32),
    "slab_sq1": ((1, ROWS), f32),
    "mine": ((2, 2, SHARES, 8, 128), f32),
    "land0": ((2, HALF_TILES, 8, 128), f32),
    "land1": ((2, 15, SHARE, 8, 128), f32),
    "mid": ((2, SHARE, 8, 128), f32),
    "land2": ((2, 7, SHARE, 8, 128), f32),
    "total": ((2, 2, SHARES, 8, 128), f32),
}


def kernel(*refs):
    m = Refs((*INPUTS, *OUTPUTS, *SCRATCH, "ss", "rs"), refs)
    s, c = lax.axis_index("src"), lax.axis_index("dst")
    core, low, z = c % 2, (c // 2) % 2, c // 4
    g = s * 2 + low
    x, y = s // 4 * 2 + low, s % 4

    def plane_index(x, y):
        return (x // 2 * 4 + y) * 2 + x % 2

    def in_plane(k):
        return (k // 2, (z * 2 + k % 2) * 2 + core)

    def along_z(k):
        return (s, (k * 2 + low) * 2 + core)

    peer = (s, c + 1 - 2 * core)
    right, left = (s, (c + 1) % 32), (s, (c + 31) % 32)

    def wait_for(ref, sem):
        pltpu.make_async_copy(ref, ref, sem).wait()

    barrier = pltpu.get_barrier_semaphore()
    for device in (
        [peer, left]
        + [in_plane((g + i) % 16) for i in range(1, 16)]
        + [along_z((z + i) % 8) for i in range(1, 8)]
    ):
        pl.semaphore_signal(barrier, inc=1, device_id=device, device_id_type=MESH)

    place_ids(m)
    m.slab_parts[...] = stacked(m.slab0[...])
    m.src_parts[...] = stacked(m.src0[...])
    m.rel_parts[...] = stacked(m.rel0[...])
    gather_negatives(0, m)
    gather_all(0, m)

    for rnd in range(ROUNDS):
        ss, rs = m.ss.at[rnd], m.rs.at[rnd]
        mine, total = m.mine.at[rnd], m.total.at[rnd]
        land0, land1, land2, mid = m.land0.at[rnd], m.land1.at[rnd], m.land2.at[rnd], m.mid.at[rnd]
        if rnd == 0:
            src, src_sq, slab, slab_sq, rel, rel_sq = m.src0, m.src_sq0, m.slab0, m.slab_sq0, m.rel0, m.rel_sq0
            new_src, new_src_sq, new_rel, new_rel_sq = m.src1, m.src_sq1, m.rel1, m.rel_sq1
        else:
            src, src_sq, slab, slab_sq, rel, rel_sq = m.src1, m.src_sq1, m.slab1, m.slab_sq1, m.rel1, m.rel_sq1
            new_src, new_src_sq, new_rel, new_rel_sq = m.src2, m.src_sq2, m.rel2, None

        def send(what, where, n, device):
            copy = pltpu.make_async_remote_copy(
                what, where, ss.at[n], rs.at[n], device_id=device, device_id_type=MESH
            )
            copy.start()
            return copy

        all_terms(m)
        rel_gradient(m, mine, 1 - core)

        if rnd == 0:
            pl.semaphore_wait(barrier, 24)
        swap = send(mine.at[1 - core, pl.ds(0, HALF_TILES)], land0, 0, peer)
        rel_gradient(m, mine, core)
        mine[core, HALF_TILES:SHARES] = jnp.zeros((SHARES - HALF_TILES, 8, 128), f32)
        swap.wait_recv()
        mine[core, 0:HALF_TILES] += land0[...]
        for i, (dx, dy) in enumerate(PLANE):
            k = plane_index((x + dx) % 4, (y + dy) % 4)
            send(mine.at[core, pl.ds(k * SHARE, SHARE)], land1.at[i], 1, in_plane(k))
        for q in range(2):
            row_update(m.slab_terms, m.slab_hot, slab, slab_sq, m.slab_new.at[rnd], m.slab_sq_new.at[rnd], q)
        hop = send(m.slab_new.at[rnd], m.slab1 if rnd == 0 else m.slab_out, 2, right)
        if rnd == 0:
            hop_sq = send(m.slab_sq_new.at[rnd], m.slab_sq1, 3, right)
        wait_for(land1, rs.at[1])
        mid[...] = mine[core, pl.ds(g * SHARE, SHARE)] + jnp.sum(land1[...], axis=0)
        for i in (4, 3, 5, 2, 6, 1, 7):
            send(mid, land2.at[i - 1], 4, along_z((z + i) % 8))
        for q in range(2):
            row_update(m.src_terms, m.src_hot, src, src_sq, new_src, new_src_sq, q)
        wait_for(land2, rs.at[4])
        part = total.at[core, pl.ds(g * SHARE, SHARE)]
        part[...] = mid[...] + jnp.sum(land2[...], axis=0)
        for dx, dy in PLANE:
            send(part, part, 5, in_plane(plane_index((x + dx) % 4, (y + dy) % 4)))
        if rnd == 0:
            hop.wait_recv()
            hop_sq.wait_recv()
            m.slab_parts[...] = stacked(m.slab1[...])
            m.src_parts[...] = stacked(m.src1[...])
            gather_negatives(1, m)
            gather_all(1, m)
        wait_for(land1, rs.at[5])
        half = total.at[core, pl.ds(0, HALF_TILES)]
        back = send(half, half, 6, peer)
        rel_update(m, core, rel, rel_sq, total, new_rel, new_rel_sq)
        back.wait_recv()
        rel_update(m, 1 - core, rel, rel_sq, total, new_rel, new_rel_sq)
        if rnd == 1:
            hop.wait_recv()
        swap.wait_send()
        wait_for(land1, ss.at[1])
        hop.wait_send()
        if rnd == 0:
            hop_sq.wait_send()
        wait_for(land2, ss.at[4])
        wait_for(land1, ss.at[5])
        back.wait_send()


def both_rounds(*args):
    vmem = pl.BlockSpec(memory_space=pltpu.VMEM)
    return pl.pallas_call(
        kernel,
        out_shape=[
            jax.ShapeDtypeStruct((D, ROWS), f32),
            jax.ShapeDtypeStruct((D, ROWS), f32),
            jax.ShapeDtypeStruct((D, REL), f32),
        ],
        in_specs=[vmem] * 11,
        out_specs=[vmem] * 3,
        scratch_shapes=[pltpu.VMEM(*of) for of in SCRATCH.values()]
        + [pltpu.SemaphoreType.DMA((2, 7)), pltpu.SemaphoreType.DMA((2, 7))],
        compiler_params=pltpu.CompilerParams(
            collective_id=0, has_side_effects=True, vmem_limit_bytes=VMEM_LIMIT
        ),
        name="both_rounds",
    )(*args)


def shards(
    src_rows,
    src_state,
    dst_rows,
    dst_state,
    relations,
    relation_state,
    block_tiles,
    src_offsets,
    dst_offsets,
    relation_ids,
    negative_ids,
):
    src, slab, rel = both_rounds(
        block_tiles.transpose(0, 2, 1),
        src_rows.T,
        src_state[None, :],
        dst_rows.T,
        dst_state[None, :],
        relations.T,
        relation_state[None, :],
        src_offsets,
        dst_offsets,
        relation_ids,
        negative_ids,
    )
    return src.T, slab.T, rel.T


def solution(mesh):
    own = ("src", "dst")
    ids = P(None, own, None)
    return jax.shard_map(
        shards,
        mesh=mesh,
        in_specs=(P(own, None), P(own), P(own, None), P(own), P(), P(), ids, ids, ids, ids, ids),
        out_specs=(P(own, None), P(own, None), P()),
        check_vma=False,
    )
```

```python
import jax
import jax.numpy as jnp
from jax import lax
from jax.experimental import pallas as pl
from jax.experimental.pallas import tpu as pltpu
from jax.sharding import PartitionSpec as P

MESH = pl.DeviceIdType.MESH
f32, bf16, i32 = jnp.float32, jnp.bfloat16, jnp.int32
learn_rate = 0.1
D, REL, TILE, NEG, ROWS, BLK, ROUNDS = 200, 1024, 128, 50, 512, 16, 2
EDGES = BLK * TILE
NEGS = BLK * 64
FEATS = D // 8
HALF_TILES = 4 * FEATS
PLANE_SHARE, LINE_SHARE = 5, 3
PLANE_TILES = 16 * PLANE_SHARE
TILES = PLANE_TILES + 8 * LINE_SHARE
VMEM_LIMIT = 60 << 20
NT = ((1,), (1,))
TN = ((0,), (0,))


def two_parts(value):
    high = value.astype(bf16)
    return high, (value - high.astype(f32)).astype(bf16)


def stacked(value):
    return jnp.concatenate(two_parts(value), axis=0)


def folded(value):
    half = value.shape[0] // 2
    return value[:half] + value[half:]


def dot(a, b, dims=((1,), (0,))):
    return lax.dot_general(a, b, (dims, ((), ())), preferred_element_type=f32)


def one_hot(ids, rows):
    places = lax.broadcasted_iota(i32, (rows, ids.shape[1]), 0)
    return jnp.where(places == ids, 1.0, 0.0).astype(bf16)


def adagrad(table, sums, grad):
    sums = sums + jnp.sum(grad * grad, axis=0, keepdims=True) * (1.0 / D)
    return table - grad * (learn_rate / jnp.sqrt(sums)), sums


def lanes_at(start, size):
    return pl.ds(start if isinstance(start, int) else pl.multiple_of(start, size), size)


def as_column(row):
    size = row.shape[1]
    square = lax.broadcasted_iota(i32, (size, size), 0) == lax.broadcasted_iota(i32, (size, size), 1)
    return jnp.sum(jnp.where(square, row.astype(f32), 0.0), axis=1, keepdims=True).astype(i32)


def place_ids(m):
    for rnd in range(ROUNDS):
        tiles = m.tiles[rnd]
        m.src_ids[rnd] = m.src_off[rnd] + as_column(tiles[0:1]) * TILE
        m.dst_ids[rnd] = m.dst_off[rnd] + as_column(tiles[1:2]) * TILE


def gather_negatives(rnd, m):
    ids = m.neg_ids[rnd]
    ids = jnp.concatenate([ids, jnp.full((BLK, 64 - NEG), -1, i32)], axis=1)
    for p in range(4):
        row = jnp.concatenate([ids[4 * p + j : 4 * p + j + 1, :] for j in range(4)], axis=1)
        hot = one_hot(row, ROWS)
        m.slab_hot[:, pl.ds(EDGES + p * 256, 256)] = hot
        negs = folded(dot(m.slab_parts[...], hot))
        here = pl.ds(p * 256, 256)
        m.neg_parts[:, here] = stacked(negs)
        for part, value in enumerate(two_parts(negs.T)):
            m.negs_turned[part, here, :] = value


def pair_ids(ref, rnd, p):
    return jnp.concatenate([ref[rnd, pl.ds(2 * p + j, 1), :] for j in range(2)], axis=1)


def gather_pair(rnd, m, p):
    both = lanes_at(p * 256, 256)
    src_hot = one_hot(pair_ids(m.src_ids, rnd, p), ROWS)
    dst_hot = one_hot(pair_ids(m.dst_ids, rnd, p), ROWS)
    m.src_hot[:, both] = src_hot
    m.slab_hot[:, both] = dst_hot
    m.heads[:, both] = folded(dot(m.src_parts[...], src_hot))
    m.tails[:, both] = folded(dot(m.slab_parts[...], dst_hot))
    m.rel_hot[:, both] = one_hot(pair_ids(m.rel_ids, rnd, p), REL)


def group_terms(m, first, count):
    pairs = range(count)
    both = [lanes_at((first + i) * 256, 256) for i in pairs]
    own = [lanes_at((first + i) * 128, 128) for i in pairs]
    lifted, parts, neg, score, weight = [], [], [], [], []
    for i in pairs:
        diagonal = folded(dot(m.rel_parts[...], m.rel_hot[:, both[i]]))
        m.diagonals[:, both[i]] = diagonal
        lifted.append(m.heads[:, both[i]] * diagonal)
        parts.append(two_parts(lifted[i]))
    for i in pairs:
        high, low = parts[i]
        turned = m.negs_turned[:, own[i], :]
        score.append(dot(turned.reshape(256, D), high))
        score[i] = folded(score[i]) + dot(turned[0], low)
    for i in pairs:
        pieces = [jax.nn.sigmoid(score[i][64 * j : 64 * j + 64, 128 * j : 128 * j + 128]) * (1.0 / NEG) for j in range(2)]
        nothing = jnp.zeros((64, 128), f32)
        weight.append(
            two_parts(
                jnp.concatenate(
                    [jnp.concatenate([pieces[0], nothing], axis=1), jnp.concatenate([nothing, pieces[1]], axis=1)], axis=0
                )
            )
        )
    for i in pairs:
        head, tail = m.heads[:, both[i]], m.tails[:, both[i]]
        negs = m.neg_parts[:, own[i]]
        positive = jnp.sum(lifted[i] * tail, axis=0, keepdims=True)
        pos_weight = -jax.nn.sigmoid(-positive)
        pulled = pos_weight * tail + folded(dot(negs, weight[i][0])) + dot(negs[:D], weight[i][1])
        m.src_terms[:, both[i]] = stacked(pulled * m.diagonals[:, both[i]])
        m.rel_terms[:, both[i]] = stacked(pulled * head)
        m.slab_terms[:, both[i]] = stacked(pos_weight * lifted[i])
    for i in pairs:
        neg_grad = folded(dot(jnp.concatenate(parts[i], axis=0), weight[i][0], NT)) + dot(parts[i][0], weight[i][1], NT)
        m.slab_terms[:, lanes_at(EDGES + (first + i) * 128, 128)] = stacked(neg_grad)


GROUP = 8


def all_terms(m):
    for i in range(BLK // 2 // GROUP):
        group_terms(m, i * GROUP, GROUP)


def gather_all(rnd, m):
    for p in range(BLK // 2):
        gather_pair(rnd, m, p)


def rel_gradient(m, out, half):
    for q in range(2):
        rows = lanes_at(half * (REL // 2) + q * 256, 256)
        grad = folded(dot(m.rel_terms[...], m.rel_hot[rows, :], NT))
        for j in range(2):
            piece = grad[:, j * 128 : j * 128 + 128]
            out[half, pl.ds((2 * q + j) * FEATS, FEATS)] = piece.reshape(FEATS, 8, 128)


def row_update(terms, hot, table, sums, new_table, new_sums, q):
    rows = pl.ds(q * 256, 256)
    grad = folded(dot(terms[...], hot[rows, :], NT))
    new_table[:, rows], new_sums[:, rows] = adagrad(table[:, rows], sums[:, rows], grad)


def rel_update(m, half, table, sums, grad, new_table, new_sums):
    for j in range(4):
        rows = lanes_at(half * (REL // 2) + j * 128, 128)
        piece = grad[half, pl.ds(j * FEATS, FEATS)].reshape(D, 128)
        new, new_sq = adagrad(table[:, rows], sums[:, rows], piece)
        new_table[:, rows] = new
        if new_sums is not None:
            new_sums[:, rows] = new_sq
            m.rel_parts[:, rows] = stacked(new)


PLANE = sorted(
    ((dx, dy) for dx in range(4) for dy in range(4) if dx or dy),
    key=lambda step: -min(step[0], 4 - step[0]) - min(step[1], 4 - step[1]),
)

LINE = (4, 3, 5, 2, 6, 1, 7)
STEPS = [
    (to_plane, i)
    for _, to_plane, i in sorted([(i / 7, False, i) for i in range(7)] + [(i / 15, True, i) for i in range(15)])
]


class Refs:
    def __init__(self, names, refs):
        for name, ref in zip(names, refs, strict=True):
            setattr(self, name, ref)


INPUTS = (
    ("tiles", "src0", "src_sq0", "slab0", "slab_sq0", "rel0", "rel_sq0")
    + ("src_off", "dst_off", "rel_ids", "neg_ids")
)
OUTPUTS = ("src2", "slab_out", "rel2")
SCRATCH = {
    "src_ids": ((ROUNDS, BLK, TILE), i32),
    "dst_ids": ((ROUNDS, BLK, TILE), i32),
    "src_parts": ((2 * D, ROWS), bf16),
    "slab_parts": ((2 * D, ROWS), bf16),
    "rel_parts": ((2 * D, REL), bf16),
    "rel_hot": ((REL, EDGES), bf16),
    "src_hot": ((ROWS, EDGES), bf16),
    "slab_hot": ((ROWS, EDGES + NEGS), bf16),
    "neg_parts": ((2 * D, NEGS), bf16),
    "negs_turned": ((2, NEGS, D), bf16),
    "diagonals": ((D, EDGES), f32),
    "heads": ((D, EDGES), f32),
    "tails": ((D, EDGES), f32),
    "src_terms": ((2 * D, EDGES), bf16),
    "slab_terms": ((2 * D, EDGES + NEGS), bf16),
    "rel_terms": ((2 * D, EDGES), bf16),
    "src1": ((D, ROWS), f32),
    "src_sq1": ((1, ROWS), f32),
    "src_sq2": ((1, ROWS), f32),
    "rel1": ((D, REL), f32),
    "rel_sq1": ((1, REL), f32),
    "slab_new": ((2, D, ROWS), f32),
    "slab_sq_new": ((2, 1, ROWS), f32),
    "slab1": ((D, ROWS), f32),
    "slab_sq1": ((1, ROWS), f32),
    "mine": ((2, 2, TILES, 8, 128), f32),
    "land0": ((2, HALF_TILES, 8, 128), f32),
    "plane_in": ((2, 15, PLANE_SHARE, 8, 128), f32),
    "line_in": ((2, 7, LINE_SHARE, 8, 128), f32),
    "plane_mid": ((2, PLANE_SHARE, 8, 128), f32),
    "line_mid": ((2, LINE_SHARE, 8, 128), f32),
    "plane_in2": ((2, 7, PLANE_SHARE, 8, 128), f32),
    "line_in2": ((2, 15, LINE_SHARE, 8, 128), f32),
    "total": ((2, 2, TILES, 8, 128), f32),
}


def kernel(*refs):
    m = Refs((*INPUTS, *OUTPUTS, *SCRATCH, "ss", "rs"), refs)
    s, c = lax.axis_index("src"), lax.axis_index("dst")
    core, low, z = c % 2, (c // 2) % 2, c // 4
    g = s * 2 + low
    x, y = s // 4 * 2 + low, s % 4

    def plane_index(x, y):
        return (x // 2 * 4 + y) * 2 + x % 2

    def in_plane(k):
        return (k // 2, (z * 2 + k % 2) * 2 + core)

    def along_z(k):
        return (s, (k * 2 + low) * 2 + core)

    peer = (s, c + 1 - 2 * core)
    right, left = (s, (c + 1) % 32), (s, (c + 31) % 32)

    def plane_of(i):
        return plane_index((x + PLANE[i][0]) % 4, (y + PLANE[i][1]) % 4)

    def line_of(i):
        return (z + LINE[i]) % 8

    def wait_for(ref, sem):
        pltpu.make_async_copy(ref, ref, sem).wait()

    barrier = pltpu.get_barrier_semaphore()
    for device in (
        [peer, left]
        + [in_plane((g + i) % 16) for i in range(1, 16)]
        + [along_z((z + i) % 8) for i in range(1, 8)]
    ):
        pl.semaphore_signal(barrier, inc=1, device_id=device, device_id_type=MESH)

    place_ids(m)
    m.slab_parts[...] = stacked(m.slab0[...])
    m.src_parts[...] = stacked(m.src0[...])
    m.rel_parts[...] = stacked(m.rel0[...])
    gather_negatives(0, m)
    gather_all(0, m)

    for rnd in range(ROUNDS):
        ss, rs = m.ss.at[rnd], m.rs.at[rnd]
        mine, total = m.mine.at[rnd], m.total.at[rnd]
        land0 = m.land0.at[rnd]
        plane_in, plane_mid, plane_in2 = m.plane_in.at[rnd], m.plane_mid.at[rnd], m.plane_in2.at[rnd]
        line_in, line_mid, line_in2 = m.line_in.at[rnd], m.line_mid.at[rnd], m.line_in2.at[rnd]
        if rnd == 0:
            src, src_sq, slab, slab_sq, rel, rel_sq = m.src0, m.src_sq0, m.slab0, m.slab_sq0, m.rel0, m.rel_sq0
            new_src, new_src_sq, new_rel, new_rel_sq = m.src1, m.src_sq1, m.rel1, m.rel_sq1
        else:
            src, src_sq, slab, slab_sq, rel, rel_sq = m.src1, m.src_sq1, m.slab1, m.slab_sq1, m.rel1, m.rel_sq1
            new_src, new_src_sq, new_rel, new_rel_sq = m.src2, m.src_sq2, m.rel2, None

        def send(what, where, n, device):
            copy = pltpu.make_async_remote_copy(
                what, where, ss.at[n], rs.at[n], device_id=device, device_id_type=MESH
            )
            copy.start()
            return copy

        all_terms(m)
        rel_gradient(m, mine, 1 - core)

        if rnd == 0:
            pl.semaphore_wait(barrier, 24)
        swap = send(mine.at[1 - core, pl.ds(0, HALF_TILES)], land0, 0, peer)
        rel_gradient(m, mine, core)
        mine[core, HALF_TILES:TILES] = jnp.zeros((TILES - HALF_TILES, 8, 128), f32)
        swap.wait_recv()
        mine[core, 0:HALF_TILES] += land0[...]
        for to_plane, i in STEPS:
            if to_plane:
                k = plane_of(i)
                send(mine.at[core, pl.ds(k * PLANE_SHARE, PLANE_SHARE)], plane_in.at[i], 1, in_plane(k))
            else:
                k = line_of(i)
                send(mine.at[core, pl.ds(PLANE_TILES + k * LINE_SHARE, LINE_SHARE)], line_in.at[i], 7, along_z(k))
        for q in range(2):
            row_update(m.slab_terms, m.slab_hot, slab, slab_sq, m.slab_new.at[rnd], m.slab_sq_new.at[rnd], q)
        hop = pltpu.make_async_remote_copy(
            m.slab_new.at[rnd],
            m.slab1 if rnd == 0 else m.slab_out,
            ss.at[2],
            rs.at[2],
            device_id=right,
            device_id_type=MESH,
        )

        @pl.when(core == 0)
        def _():
            hop.start()

        if rnd == 0:
            hop_sq = send(m.slab_sq_new.at[rnd], m.slab_sq1, 3, right)
        own_plane = pl.ds(g * PLANE_SHARE, PLANE_SHARE)
        own_line = pl.ds(PLANE_TILES + z * LINE_SHARE, LINE_SHARE)
        wait_for(line_in, rs.at[7])
        line_mid[...] = mine[core, own_line] + jnp.sum(line_in[...], axis=0)
        for i in range(15):
            send(line_mid, line_in2.at[i], 8, in_plane(plane_of(i)))
        wait_for(plane_in, rs.at[1])
        plane_mid[...] = mine[core, own_plane] + jnp.sum(plane_in[...], axis=0)
        for i in range(7):
            send(plane_mid, plane_in2.at[i], 4, along_z(line_of(i)))

        @pl.when(core == 1)
        def _():
            hop.start()

        for q in range(2):
            row_update(m.src_terms, m.src_hot, src, src_sq, new_src, new_src_sq, q)
        plane_part, line_part = total.at[core, own_plane], total.at[core, own_line]
        wait_for(line_in2, rs.at[8])
        line_part[...] = line_mid[...] + jnp.sum(line_in2[...], axis=0)
        for i in range(7):
            send(line_part, line_part, 9, along_z(line_of(i)))
        wait_for(plane_in2, rs.at[4])
        plane_part[...] = plane_mid[...] + jnp.sum(plane_in2[...], axis=0)
        for i in range(15):
            send(plane_part, plane_part, 5, in_plane(plane_of(i)))
        if rnd == 0:
            hop.wait_recv()
            hop_sq.wait_recv()
            m.slab_parts[...] = stacked(m.slab1[...])
            m.src_parts[...] = stacked(m.src1[...])
            gather_negatives(1, m)
            gather_all(1, m)
        wait_for(line_in, rs.at[9])
        wait_for(plane_in, rs.at[5])
        half = total.at[core, pl.ds(0, HALF_TILES)]
        back = send(half, half, 6, peer)
        rel_update(m, core, rel, rel_sq, total, new_rel, new_rel_sq)
        back.wait_recv()
        rel_update(m, 1 - core, rel, rel_sq, total, new_rel, new_rel_sq)
        if rnd == 1:
            hop.wait_recv()
        swap.wait_send()
        wait_for(plane_in, ss.at[1])
        wait_for(line_in, ss.at[7])
        hop.wait_send()
        if rnd == 0:
            hop_sq.wait_send()
        wait_for(plane_in2, ss.at[4])
        wait_for(line_in2, ss.at[8])
        wait_for(plane_in, ss.at[5])
        wait_for(line_in, ss.at[9])
        back.wait_send()


def both_rounds(*args):
    vmem = pl.BlockSpec(memory_space=pltpu.VMEM)
    return pl.pallas_call(
        kernel,
        out_shape=[
            pltpu.VMEM((D, ROWS), f32),
            pltpu.VMEM((D, ROWS), f32),
            pltpu.VMEM((D, REL), f32),
        ],
        in_specs=[vmem] * 11,
        out_specs=[vmem] * 3,
        scratch_shapes=[pltpu.VMEM(*of) for of in SCRATCH.values()]
        + [pltpu.SemaphoreType.DMA((2, 10)), pltpu.SemaphoreType.DMA((2, 10))],
        compiler_params=pltpu.CompilerParams(
            collective_id=0, has_side_effects=True, vmem_limit_bytes=VMEM_LIMIT
        ),
        name="both_rounds",
    )(*args)


def settle_kernel(*refs):
    copies = [pltpu.make_async_copy(refs[i], refs[3 + i], refs[6].at[i]) for i in range(3)]
    for copy in copies:
        copy.start()
    for copy in copies:
        copy.wait()


def settle(*arrays):
    arrays = [pltpu.with_memory_space_constraint(a, pltpu.VMEM) for a in arrays]
    anywhere = pl.BlockSpec(memory_space=pl.ANY)
    return pl.pallas_call(
        settle_kernel,
        out_shape=[jax.ShapeDtypeStruct(a.shape, a.dtype) for a in arrays],
        in_specs=[pl.BlockSpec(memory_space=pltpu.VMEM)] * 3,
        out_specs=[anywhere] * 3,
        scratch_shapes=[pltpu.SemaphoreType.DMA((3,))],
        compiler_params=pltpu.CompilerParams(vmem_limit_bytes=8 << 20),
        name="settle",
    )(*arrays)


def shards(
    src_rows,
    src_state,
    dst_rows,
    dst_state,
    relations,
    relation_state,
    block_tiles,
    src_offsets,
    dst_offsets,
    relation_ids,
    negative_ids,
):
    results = both_rounds(
        block_tiles.transpose(0, 2, 1),
        src_rows.T,
        src_state[None, :],
        dst_rows.T,
        dst_state[None, :],
        relations.T,
        relation_state[None, :],
        src_offsets,
        dst_offsets,
        relation_ids,
        negative_ids,
    )
    src, slab, rel = settle(*results)
    return src.T, slab.T, rel.T


def solution(mesh):
    own = ("src", "dst")
    ids = P(None, own, None)
    return jax.shard_map(
        shards,
        mesh=mesh,
        in_specs=(P(own, None), P(own), P(own, None), P(own), P(), P(), ids, ids, ids, ids, ids),
        out_specs=(P(own, None), P(own, None), P()),
        check_vma=False,
    )
```
